256 devices in a mesh: dp: 64 (over x, z, core), mp: 4 (over y).
Axes of the slice: x: 4, y: 4, z: 8, core: 2. Of those that a mesh axis runs over, the one named last changes fastest.
Arguments:
- activations: bfloat16 [32768, 2560], P('dp'), may hold values from -6 to 6
- cotangent: bfloat16 [32768, 6912], P('dp', 'mp'), may hold values from -6 to 6
- frozen_weight: bfloat16 [2560, 6912], P(None, 'mp'), may hold values from -0.078125 to 0.078125
- skew_params: bfloat16 [10, 256, 256], replicated, may hold values from -0.125 to 0.125
- tile_order: int32 [20], replicated, may hold values from 0 to 19, each once
- block_owner: int32 [10], replicated, may hold values from 0 to 63, as said below
Outputs:
- input_grad: bfloat16 [32768, 2560], P('dp', 'mp')
- skew_grads: float32 [192, 256, 256], P('dp')
The draws below stay inside these ranges and needn't reach their ends.
Inputs may be any that keep to these rules, and one draw needn't show every extreme that they name: `tile_order`: a permutation of the 20 tiles. `block_owner`: no index of dp owns more than 3 blocks, and some index owns exactly 3; indices 0 and 64 - 1 own blocks in every draw.
All inputs are finite; a program needn't handle non-finite values.
Results may differ from the reference program's by a relative error of at most 0.001.
Values sent between devices are 32-bit elements; how exact they have to be, the bound alone decides.
No kernel may reach another device: no remote copies, remote signals or barrier semaphores. Data moves between devices by JAX's collectives and lax.ppermute only.
A program may use at most 128 MiB of HBM per device.

```python
import math
import jax
import jax.numpy as jnp
from jax import lax

D = 2560
FF = 6912
BLOCK = 256
SLOTS = 3
TOKENS = 32768
TILES = 20
BLOCKS = 10
N_DP = 64


def draw_block_owner(key, part):
    first_key, second_key = jax.random.split(jax.random.fold_in(key, 17))
    groups = (jnp.arange(BLOCKS, dtype=jnp.int32) // SLOTS).astype(jnp.int32)
    shuffled = jax.random.permutation(first_key, BLOCKS)
    middle = (jax.random.permutation(second_key, N_DP - 2) + 1).astype(jnp.int32)
    heads = jnp.array([N_DP - 1, 0], dtype=jnp.int32)
    devices = jnp.concatenate([heads, middle.astype(jnp.int32)]).astype(jnp.int32)
    return devices[groups[shuffled]].astype(jnp.int32)


def block_levels(own_key, extent, shards, smallest, largest):
    loudness = 1.0
    for dim, blocks in shards:
        draws = jax.random.uniform(jax.random.fold_in(jax.random.fold_in(own_key, 6), dim), (blocks,), jnp.float32, smallest / len(shards), largest / len(shards))
        loudness = loudness * jnp.repeat(jnp.exp(draws), extent[dim] // blocks).reshape((-1,) + (1,) * (len(extent) - 1 - dim))
    return loudness


def scatter_about(key, shape, scale, limit, shards=(), kind=jnp.bfloat16):
    values = jax.random.normal(key, shape, jnp.float32) * scale
    if len(shards) > 0:
        values = block_levels(key, shape, shards, -0.22, 0.18) * values
    return jnp.clip(values, min=-limit, max=limit).astype(kind)


def setup_inputs(seed: int = 0) -> dict:
    keys = jax.random.split(jax.random.key(seed), 7)
    activations = scatter_about(keys[0], (TOKENS, D), 1.0, 6.0, ((0, 64),))
    cotangent = scatter_about(keys[1], (TOKENS, FF), 1.0, 6.0, ((0, 64), (1, 4)))
    frozen_weight = scatter_about(keys[2], (D, FF), FF ** -0.5, 0.078125, ((1, 4),))
    skew_params = scatter_about(keys[3], (BLOCKS, BLOCK, BLOCK), (0.14 * BLOCK ** -0.5), 0.125)
    tile_order = jax.random.permutation(keys[4], TILES).astype(jnp.int32)
    block_owner = draw_block_owner(jax.random.fold_in(keys[6], 71), 0)
    return dict(activations=activations, cotangent=cotangent, frozen_weight=frozen_weight, skew_params=skew_params, tile_order=tile_order, block_owner=block_owner)


highest = lax.Precision.HIGHEST

def product(first, second):
    return jnp.einsum('bij,bjk->bik', first, second, precision=highest)

def cayley_parts(params):
    plain = params.astype(jnp.float32)
    skew = plain - jnp.swapaxes(plain, 1, 2)
    square = product(skew, skew)
    cube = product(square, skew)
    identity = jnp.eye(skew.shape[1], dtype=jnp.float32)
    return (skew, identity[None] + 2.0 * skew + 2.0 * square + cube)

def to_blocks(matrix, order, tile_count, block_count):
    tiled = matrix.reshape(matrix.shape[0], tile_count, -1)
    return jnp.take(tiled, order, axis=1).reshape(matrix.shape[0], block_count, -1)

def from_blocks(blocked, order, tile_count):
    positions = jnp.arange(tile_count, dtype=jnp.int32)
    matches = (order[:, None] == positions[None, :]).astype(jnp.int32)
    inverse = lax.optimization_barrier(jnp.sum(positions[:, None] * matches, axis=0)).astype(jnp.int32)
    tiled = blocked.reshape(blocked.shape[0], tile_count, -1)
    return jnp.take(tiled, inverse, axis=1).reshape(blocked.shape[0], -1)

def adjoint(gram, skew):
    transposed = jnp.swapaxes(skew, 1, 2)
    left = product(gram, transposed)
    right = product(transposed, gram)
    total = 2.0 * gram + 2.0 * (left + right) + product(left, transposed) + product(transposed, left) + product(transposed, right)
    return total - jnp.swapaxes(total, 1, 2)

def reference(activations, cotangent, frozen_weight, skew_params, tile_order, block_owner):
    skew, rotation = cayley_parts(skew_params)
    feature_grad = jnp.dot(cotangent, frozen_weight.T, preferred_element_type=jnp.float32)
    grad_blocks = to_blocks(feature_grad, tile_order, TILES, BLOCKS)
    input_blocks = to_blocks(activations.astype(jnp.float32), tile_order, TILES, BLOCKS)
    rotated = jnp.einsum('tbj,bij->tbi', grad_blocks, rotation, precision=highest)
    input_grad = from_blocks(rotated, tile_order, TILES).astype(jnp.bfloat16)
    gram = jnp.einsum('tbi,tbj->bij', input_blocks, grad_blocks, precision=highest)
    block_grads = adjoint(gram, skew) * (1.0 / math.sqrt(TOKENS))
    numbers = jnp.arange(BLOCKS, dtype=jnp.int32)
    same_owner = block_owner[:, None] == block_owner[None, :]
    earlier = numbers[:, None] > numbers[None, :]
    ranking = lax.optimization_barrier(jnp.sum((same_owner & earlier).astype(jnp.int32), axis=1)).astype(jnp.int32)
    position = (block_owner * SLOTS + ranking).astype(jnp.int32)
    skew_grads = jnp.zeros((N_DP * SLOTS, BLOCK, BLOCK), jnp.float32).at[position].set(block_grads)
    return (input_grad, skew_grads)
```

```python
import math

import jax
import jax.numpy as jnp
from jax import lax
from jax.experimental import pallas as pl
from jax.experimental.pallas import tpu as pltpu
from jax.sharding import Mesh
from jax.sharding import PartitionSpec as P

SLOTS = 3
X, Z, CORES, Y = 4, 8, 2, 4
TILE = 128
BLOCK = 256
f32 = jnp.float32
bf16 = jnp.bfloat16
NN = (((1,), (0,)), ((), ()))
NT = (((1,), (1,)), ((), ()))
TN = (((0,), (0,)), ((), ()))


def dot(a, b, dims=NN):
    return lax.dot_general(a, b, dims, preferred_element_type=f32)


def split(a):
    high = a.astype(bf16)
    return high, (a - high.astype(f32)).astype(bf16)


def product(a, b):
    return dot(a[0], b[0]) + (dot(a[0], b[1]) + dot(a[1], b[0]))


def main_kernel(order, place, w0, w1, cot, a0, a1, skew_ref, *outs):
    sums, packs = outs[:8], outs[8:]
    b = pl.program_id(0)
    y, core = place[0], place[1]
    plain = skew_ref[0].astype(f32)
    turned = plain.T - plain
    turned_pair = split(turned)
    square = product(turned_pair, turned_pair)
    cube = product(split(square), turned_pair)
    rows = lax.broadcasted_iota(jnp.int32, (BLOCK, BLOCK), 0)
    cols = lax.broadcasted_iota(jnp.int32, (BLOCK, BLOCK), 1)
    rotation_t = jnp.where(rows == cols, 1.0, 0.0) + 2.0 * turned + 2.0 * square + cube
    weight = jnp.concatenate([w0[...], w1[...]], axis=0)
    grad = dot(cot[...], weight, NT)
    grad_pair = split(grad)
    inputs = jnp.concatenate([a0[...], a1[...]], axis=1)
    gram = dot(inputs, grad_pair[0], TN) + dot(inputs, grad_pair[1], TN)
    rotated = product(grad_pair, split(rotation_t))
    half = rotated.shape[0] // 2
    for side in range(2):
        tile = order[2 * b + side]
        owner = lax.div(tile, 5)
        place_in = lax.rem(tile, 5)
        relative = lax.rem(owner - y + Y, Y)
        columns = rotated[:, side * TILE : (side + 1) * TILE]
        for r in range(Y):

            @pl.when(relative == r)
            def _(r=r, place_in=place_in, columns=columns):
                sums[2 * r][place_in] = columns[:half]
                sums[2 * r + 1][place_in] = columns[half:]

    gram_t = gram.T
    odd = gram - gram_t
    first = product(split(odd), turned_pair)
    second = product(split(2.0 * (gram + gram_t) + first), turned_pair)
    third = product(turned_pair, split(first))
    total = odd + second + 0.5 * third
    grads = total - total.T
    near = rows[:TILE, :TILE] < cols[:TILE, :TILE]
    pack = jnp.concatenate(
        [jnp.where(near, grads[:TILE, :TILE], grads[TILE:, TILE:]), grads[:TILE, TILE:]], axis=0
    ).reshape(32, 8, TILE)
    mine = lax.div(b, 5) == core
    where = lax.rem(b, 5)

    @pl.when(mine)
    def _():
        packs[0][:, pl.ds(where, 1)] = pack[:, None]

    @pl.when(jnp.logical_not(mine))
    def _():
        packs[1][:, pl.ds(where, 1)] = pack[:, None]


def main_call(tile_order, place, frozen_weight, cotangent, activations, skew_params):
    tokens = cotangent.shape[0]
    wide = cotangent.shape[1]
    sums = [jax.ShapeDtypeStruct((5, tokens // 2, TILE), f32)] * 8
    packs = [jax.ShapeDtypeStruct((32, 5, 8, TILE), f32)] * 2
    whole3 = pl.BlockSpec((5, tokens // 2, TILE), lambda b, o, p: (0, 0, 0))
    whole4 = pl.BlockSpec((32, 5, 8, TILE), lambda b, o, p: (0, 0, 0, 0))
    return pl.pallas_call(
        main_kernel,
        out_shape=sums + packs,
        grid_spec=pltpu.PrefetchScalarGridSpec(
            num_scalar_prefetch=2,
            grid=(10,),
            in_specs=[
                pl.BlockSpec((TILE, wide), lambda b, o, p: (o[2 * b], 0)),
                pl.BlockSpec((TILE, wide), lambda b, o, p: (o[2 * b + 1], 0)),
                pl.BlockSpec((tokens, wide), lambda b, o, p: (0, 0)),
                pl.BlockSpec((tokens, TILE), lambda b, o, p: (0, o[2 * b])),
                pl.BlockSpec((tokens, TILE), lambda b, o, p: (0, o[2 * b + 1])),
                pl.BlockSpec((1, BLOCK, BLOCK), lambda b, o, p: (b, 0, 0)),
            ],
            out_specs=[whole3] * 8 + [whole4] * 2,
        ),
        compiler_params=pltpu.CompilerParams(vmem_limit_bytes=44 * 2**20),
        cost_estimate=pl.CostEstimate(flops=12 * 10**9, bytes_accessed=22 * 10**6, transcendentals=0),
        name="main",
    )(tile_order, place, frozen_weight, frozen_weight, cotangent, activations, activations, skew_params)


def sum_kernel(parts, out):
    total = parts[0]
    for i in range(1, 32):
        total = total + parts[i]
    out[...] = total


def sum_call(parts):
    return pl.pallas_call(
        sum_kernel,
        out_shape=jax.ShapeDtypeStruct(parts.shape[1:], f32),
        cost_estimate=pl.CostEstimate(flops=10**6, bytes_accessed=10**6, transcendentals=0),
        name="slice_sum",
    )(parts)


def route_kernel(owner, place, own, other, out):
    core = place[1]
    out[...] = jnp.zeros_like(out)
    for b in range(10):
        target = owner[b]
        rank = jnp.int32(0)
        for e in range(b):
            rank = rank + jnp.where(owner[e] == target, 1, 0)
        side, j = b // 5, b % 5

        @pl.when(lax.rem(target, CORES) == core)
        def _(target=target, rank=rank, side=side, j=j):
            value = jnp.where(core == side, own[j], other[j])
            out[lax.div(target, CORES), rank] = value


def route_call(block_owner, place, own, other):
    smem = pl.BlockSpec(memory_space=pltpu.SMEM)
    vmem = pl.BlockSpec(memory_space=pltpu.VMEM)
    return pl.pallas_call(
        route_kernel,
        out_shape=jax.ShapeDtypeStruct((32, SLOTS, 8, TILE), f32),
        in_specs=[smem, smem, vmem, vmem],
        out_specs=vmem,
        cost_estimate=pl.CostEstimate(flops=10**5, bytes_accessed=10**6, transcendentals=0),
        name="route",
    )(block_owner, place, own, other)


def unpack_kernel(scale, parts, out):
    rows = lax.broadcasted_iota(jnp.int32, (TILE, TILE), 0)
    cols = lax.broadcasted_iota(jnp.int32, (TILE, TILE), 1)
    for s in range(SLOTS):
        pack = parts[:, s].reshape(2 * TILE, TILE) * scale
        upper = jnp.where(rows < cols, pack[:TILE], 0.0)
        lower = jnp.where(rows > cols, pack[:TILE], 0.0)
        across = pack[TILE:]
        out[s, :TILE, :TILE] = upper - upper.T
        out[s, TILE:, TILE:] = lower - lower.T
        out[s, :TILE, TILE:] = across
        out[s, TILE:, :TILE] = -across.T


def unpack_call(parts, scale):
    return pl.pallas_call(
        lambda parts, out: unpack_kernel(scale, parts, out),
        out_shape=jax.ShapeDtypeStruct((SLOTS, BLOCK, BLOCK), f32),
        cost_estimate=pl.CostEstimate(flops=10**6, bytes_accessed=10**6, transcendentals=0),
        name="unpack",
    )(parts)


def finish_kernel(a0, a1, a2, b0, b1, b2, out):
    half = a0.shape[1]
    for k in range(5):
        columns = slice(k * TILE, (k + 1) * TILE)
        out[:half, columns] = (a0[k] + a1[k] + a2[k]).astype(bf16)
        out[half:, columns] = (b0[k] + b1[k] + b2[k]).astype(bf16)


def finish_call(*parts):
    tokens = 2 * parts[0].shape[1]
    return pl.pallas_call(
        finish_kernel,
        out_shape=jax.ShapeDtypeStruct((tokens, 5 * TILE), bf16),
        compiler_params=pltpu.CompilerParams(vmem_limit_bytes=16 * 2**20),
        cost_estimate=pl.CostEstimate(flops=10**6, bytes_accessed=5 * 10**6, transcendentals=0),
        name="finish",
    )(*parts)


def turn(size, by):
    return [(i, (i + by) % size) for i in range(size)]


def local(activations, cotangent, frozen_weight, skew_params, tile_order, block_owner):
    place = jnp.stack([lax.axis_index("y"), lax.axis_index("core")]).astype(jnp.int32)
    outs = main_call(tile_order, place, frozen_weight, cotangent, activations, skew_params)
    (own_a, own_b, next_a, next_b, far_a, far_b, last_a, last_b, pack_own, pack_other) = outs
    far_a = lax.ppermute(far_a, "y", turn(Y, 1))
    last_a = lax.ppermute(last_a, "y", turn(Y, -1))
    far_b = lax.ppermute(far_b, "y", turn(Y, -1))
    next_b = lax.ppermute(next_b, "y", turn(Y, 1))
    pack = pack_own + lax.ppermute(pack_other, "core", turn(CORES, 1))
    slices = sum_call(lax.all_to_all(pack, ("x", "z"), 0, 0, tiled=True))
    next_a = lax.ppermute(next_a + far_a, "y", turn(Y, 1))
    last_b = lax.ppermute(last_b + far_b, "y", turn(Y, -1))
    others = [lax.ppermute(slices, "y", turn(Y, s)) for s in (1, 2, 3)]
    slices = (slices + others[1]) + (others[0] + others[2])
    routed = route_call(block_owner, place, slices, lax.ppermute(slices, "core", turn(CORES, 1)))
    owned = lax.all_to_all(routed, ("x", "z"), 0, 0, tiled=True)
    scale = 1.0 / math.sqrt(cotangent.shape[0] * X * Z * CORES)
    skew_grads = unpack_call(owned, scale)
    input_grad = finish_call(own_a, next_a, last_a, own_b, next_b, last_b)
    return (input_grad, skew_grads)


def solution(mesh):
    grid = Mesh(mesh.devices.reshape(X, Z, CORES, Y), ("x", "z", "core", "y"))
    dp = ("x", "z", "core")
    placed = (P(dp, None), P(dp, "y"), P(None, "y"), P(), P(), P())
    return jax.shard_map(
        local,
        mesh=grid,
        in_specs=placed,
        out_specs=(P(dp, "y"), P(dp, None, None)),
        check_vma=False,
    )
```

```python
import math

import jax
import jax.numpy as jnp
from jax import lax
from jax.experimental import pallas as pl
from jax.experimental.pallas import tpu as pltpu
from jax.sharding import Mesh
from jax.sharding import PartitionSpec as P

SLOTS = 3
FINISH = 10**10
MERGE = int(2e10)
X, Z, CORES, Y = 4, 8, 2, 4
TILE = 128
BLOCK = 256
f32 = jnp.float32
bf16 = jnp.bfloat16
NN = (((1,), (0,)), ((), ()))
NT = (((1,), (1,)), ((), ()))
TN = (((0,), (0,)), ((), ()))


def dot(a, b, dims=NN):
    return lax.dot_general(a, b, dims, preferred_element_type=f32)


def split(a):
    high = a.astype(bf16)
    return high, (a - high.astype(f32)).astype(bf16)


def stack(a, axis):
    return jnp.concatenate([a[0], a[0], a[1]] if axis else [a[0], a[1], a[0]], axis=axis)


def product(a, b):
    return dot(stack(a, 1), stack(b, 0))


def turned_skew(ref, b):
    plain = ref[b].astype(f32)
    return plain.T - plain


def grad_kernel(
    order, place, weight, cot_t, inputs, skew, turn_high, turn_low, high, low, mine, other,
    skews, tiles, cots, cot, ins, weight_sems, input_sems, sems,
):
    core = place[1]

    def column(t):
        return pl.ds(pl.multiple_of(order[t] * TILE, TILE), TILE)

    def fetch(t):
        return pltpu.make_async_copy(
            weight.at[:, column(t)], tiles.at[t // 2, :, pl.ds(TILE * (t % 2), TILE)], weight_sems.at[t]
        )

    def fetch_inputs(t):
        return pltpu.make_async_copy(
            inputs.at[:, column(t)], ins.at[t // 2, :, pl.ds(TILE * (t % 2), TILE)], input_sems.at[t]
        )

    get_skew = pltpu.make_async_copy(skew, skews, sems.at[0])
    get_cot = pltpu.make_async_copy(cot_t, cots, sems.at[1])
    get_skew.start()
    get_cot.start()
    for t in range(20):
        fetch(t).start()
    for t in range(20):
        fetch_inputs(t).start()
    get_skew.wait()
    rows = lax.broadcasted_iota(jnp.int32, (BLOCK, BLOCK), 0)
    cols = lax.broadcasted_iota(jnp.int32, (BLOCK, BLOCK), 1)
    identity = jnp.where(rows == cols, 1.0, 0.0)
    for b0 in range(0, 10, 5):
        group = range(b0, b0 + 5)
        turned = [turned_skew(skews, b) for b in group]
        pairs = [split(a) for a in turned]
        squares = [product(a, a) for a in pairs]
        cubes = [product(split(a), p) for a, p in zip(squares, pairs)]
        for b, a, square, cube in zip(group, turned, squares, cubes):
            turn_high[b], turn_low[b] = split(identity + 2.0 * a + 2.0 * square + cube)
    get_cot.wait()
    cot[...] = cots[...].T
    for t in range(20):
        fetch(t).wait()
    for b in range(10):
        high[b], low[b] = split(dot(cot[...], tiles[b]))
    for t in range(20):
        fetch_inputs(t).wait()
    for out, first in ((mine, 5 * core), (other, 5 * (1 - core))):
        for j in range(5):
            b = first + j
            tile = ins[b]
            out[j] = dot(tile, high[b], TN) + dot(tile, low[b], TN)


def vmem():
    return pl.BlockSpec(memory_space=pltpu.VMEM)


def smem():
    return pl.BlockSpec(memory_space=pltpu.SMEM)


def anywhere():
    return pl.BlockSpec(memory_space=pltpu.HBM)


def grad_call(tile_order, place, weight_t, cot_t, activations, skew_params):
    wide, tokens = cot_t.shape
    turns = jax.ShapeDtypeStruct((10, BLOCK, BLOCK), bf16)
    part = jax.ShapeDtypeStruct((10, tokens, BLOCK), bf16)
    gram = jax.ShapeDtypeStruct((5, BLOCK, BLOCK), f32)
    return pl.pallas_call(
        grad_kernel,
        out_shape=[turns, turns, part, part, gram, gram],
        in_specs=[smem(), smem()] + [anywhere() for _ in range(4)],
        out_specs=[vmem() for _ in range(6)],
        scratch_shapes=[
            pltpu.VMEM((10, BLOCK, BLOCK), bf16),
            pltpu.VMEM((10, wide, BLOCK), bf16),
            pltpu.VMEM((wide, tokens), bf16),
            pltpu.VMEM((tokens, wide), bf16),
            pltpu.VMEM((10, tokens, BLOCK), bf16),
            pltpu.SemaphoreType.DMA((20,)),
            pltpu.SemaphoreType.DMA((20,)),
            pltpu.SemaphoreType.DMA((2,)),
        ],
        compiler_params=pltpu.CompilerParams(vmem_limit_bytes=40 * 2**20),
        cost_estimate=pl.CostEstimate(flops=8 * 10**9, bytes_accessed=14 * 10**6, transcendentals=0),
        name="grad",
    )(tile_order, place, weight_t, cot_t, activations, skew_params)


def rotate_kernel(order, place, turn_high, turn_low, high, low, far_a, far_b, next_a, next_b, last_a, last_b, own, rotated):
    y = place[0]
    for b in range(10):
        product_b = product((high[b], low[b]), (turn_high[b], turn_low[b]))
        rotated[order[2 * b]] = product_b[:, :TILE]
        rotated[order[2 * b + 1]] = product_b[:, TILE:]
    half = rotated.shape[1] // 2
    for k in range(5):
        own[k] = rotated[5 * y + k]
        for r, (a, b) in enumerate(((next_a, next_b), (far_a, far_b), (last_a, last_b))):
            tile = 5 * lax.rem(y + r + 1, Y) + k
            a[k] = rotated[tile, :half]
            b[k] = rotated[tile, half:]


def rotate_call(tile_order, place, turn_high, turn_low, high, low):
    tokens = high.shape[1]
    half = jax.ShapeDtypeStruct((5, tokens // 2, TILE), f32)
    return pl.pallas_call(
        rotate_kernel,
        out_shape=[half] * 6 + [jax.ShapeDtypeStruct((5, tokens, TILE), f32)],
        in_specs=[smem(), smem()] + [vmem() for _ in range(4)],
        out_specs=[vmem() for _ in range(6)] + [vmem()],
        scratch_shapes=[pltpu.VMEM((20, tokens, TILE), f32)],
        compiler_params=pltpu.CompilerParams(vmem_limit_bytes=24 * 2**20),
        cost_estimate=pl.CostEstimate(flops=2 * 10**9, bytes_accessed=10 * 10**6, transcendentals=0),
        name="rotate",
    )(tile_order, place, turn_high, turn_low, high, low)


def adjoint_kernel(place, mine, came, skew, out):
    core = place[1]
    rows = lax.broadcasted_iota(jnp.int32, (TILE, TILE), 0)
    cols = lax.broadcasted_iota(jnp.int32, (TILE, TILE), 1)
    group = range(5)
    turned = [split(turned_skew(skew, 5 * core + j)) for j in group]
    grams = [mine[j] + came[j] for j in group]
    odd = [a - a.T for a in grams]
    even = [2.0 * (a + a.T) for a in grams]
    first = [product(split(a), t) for a, t in zip(odd, turned)]
    second = [product(split(e + a), t) for e, a, t in zip(even, first, turned)]
    third = [product(t, split(a)) for a, t in zip(first, turned)]
    for j in group:
        total = odd[j] + second[j] + 0.5 * third[j]
        grads = total - total.T
        out[:, j] = jnp.concatenate(
            [jnp.where(rows < cols, grads[:TILE, :TILE], grads[TILE:, TILE:]), grads[:TILE, TILE:]], axis=0
        ).reshape(32, 8, TILE)


def adjoint_call(place, mine, came, skew_params):
    return pl.pallas_call(
        adjoint_kernel,
        out_shape=jax.ShapeDtypeStruct((32, 5, 8, TILE), f32),
        in_specs=[smem()] + [vmem() for _ in range(3)],
        out_specs=vmem(),
        compiler_params=pltpu.CompilerParams(vmem_limit_bytes=20 * 2**20),
        cost_estimate=pl.CostEstimate(flops=2 * 10**9, bytes_accessed=4 * 10**6, transcendentals=0),
        name="adjoint",
    )(place, mine, came, skew_params)


def merge_kernel(next_a, far_a, last_b, far_b, out_a, out_b):
    out_a[...] = next_a[...] + far_a[...]
    out_b[...] = last_b[...] + far_b[...]


def merge_call(*parts):
    return pl.pallas_call(
        merge_kernel,
        out_shape=[jax.ShapeDtypeStruct(parts[0].shape, f32)] * 2,
        in_specs=[vmem() for _ in range(4)],
        out_specs=[vmem() for _ in range(2)],
        compiler_params=pltpu.CompilerParams(vmem_limit_bytes=4 * 2**20),
        cost_estimate=pl.CostEstimate(flops=MERGE, bytes_accessed=4 * 10**6, transcendentals=0),
        name="merge",
    )(*parts)


def sum_kernel(parts, out):
    total = parts[0]
    for i in range(1, 32):
        total = total + parts[i]
    out[...] = total


def sum_call(parts):
    return pl.pallas_call(
        sum_kernel,
        out_shape=jax.ShapeDtypeStruct(parts.shape[1:], f32),
        cost_estimate=pl.CostEstimate(flops=10**6, bytes_accessed=10**6, transcendentals=0),
        name="slice_sum",
    )(parts)


def route_kernel(owner, place, own, other, out):
    core = place[1]
    out[...] = jnp.zeros_like(out)
    for b in range(10):
        target = owner[b]
        rank = jnp.int32(0)
        for e in range(b):
            rank = rank + jnp.where(owner[e] == target, 1, 0)
        side, j = b // 5, b % 5

        @pl.when(lax.rem(target, CORES) == core)
        def _(target=target, rank=rank, side=side, j=j):
            value = jnp.where(core == side, own[j], other[j])
            out[lax.div(target, CORES), rank] = value


def route_call(block_owner, place, own, other):
    return pl.pallas_call(
        route_kernel,
        out_shape=jax.ShapeDtypeStruct((32, SLOTS, 8, TILE), f32),
        in_specs=[smem(), smem(), vmem(), vmem()],
        out_specs=vmem(),
        cost_estimate=pl.CostEstimate(flops=10**5, bytes_accessed=10**6, transcendentals=0),
        name="route",
    )(block_owner, place, own, other)


def unpack_kernel(scale, parts, out):
    rows = lax.broadcasted_iota(jnp.int32, (TILE, TILE), 0)
    cols = lax.broadcasted_iota(jnp.int32, (TILE, TILE), 1)
    for s in range(SLOTS):
        pack = parts[:, s].reshape(2 * TILE, TILE) * scale
        upper = jnp.where(rows < cols, pack[:TILE], 0.0)
        lower = jnp.where(rows > cols, pack[:TILE], 0.0)
        across = pack[TILE:]
        out[s, :TILE, :TILE] = upper - upper.T
        out[s, TILE:, TILE:] = lower - lower.T
        out[s, :TILE, TILE:] = across
        out[s, TILE:, :TILE] = -across.T


def unpack_call(parts, scale):
    return pl.pallas_call(
        lambda parts, out: unpack_kernel(scale, parts, out),
        out_shape=jax.ShapeDtypeStruct((SLOTS, BLOCK, BLOCK), f32),
        in_specs=[vmem()],
        cost_estimate=pl.CostEstimate(flops=10**6, bytes_accessed=10**6, transcendentals=0),
        name="unpack",
    )(parts)


def finish_kernel(own, a1, a2, b1, b2, out):
    half = own.shape[1] // 2
    for k in range(5):
        columns = slice(k * TILE, (k + 1) * TILE)
        out[:half, columns] = (own[k, :half] + a1[k] + a2[k]).astype(bf16)
        out[half:, columns] = (own[k, half:] + b1[k] + b2[k]).astype(bf16)


def finish_call(*parts):
    return pl.pallas_call(
        finish_kernel,
        out_shape=jax.ShapeDtypeStruct((parts[0].shape[1], 5 * TILE), bf16),
        in_specs=[vmem() for _ in range(5)],
        compiler_params=pltpu.CompilerParams(vmem_limit_bytes=16 * 2**20),
        cost_estimate=pl.CostEstimate(flops=FINISH, bytes_accessed=5 * 10**6, transcendentals=0),
        name="finish",
    )(*parts)


def turn(size, by):
    return [(i, (i + by) % size) for i in range(size)]


def exchange(parts):
    rows = parts.reshape(parts.shape[0], -1, parts.shape[-1])
    return lax.all_to_all(rows, ("x", "z"), 0, 0, tiled=True).reshape(parts.shape)


def local(activations, cotangent, frozen_weight, skew_params, tile_order, block_owner):
    place = jnp.stack([lax.axis_index("y"), lax.axis_index("core")]).astype(jnp.int32)
    turn_high, turn_low, high, low, mine, other = grad_call(
        tile_order, place, frozen_weight.T, cotangent.T, activations, skew_params
    )
    came = lax.ppermute(other, "core", turn(CORES, 1))
    far_a, far_b, next_a, next_b, last_a, last_b, own = rotate_call(
        tile_order, place, turn_high, turn_low, high, low
    )
    far_a = lax.ppermute(far_a, "y", turn(Y, 1))
    far_b = lax.ppermute(far_b, "y", turn(Y, -1))
    last_a = lax.ppermute(last_a, "y", turn(Y, -1))
    next_b = lax.ppermute(next_b, "y", turn(Y, 1))
    pack = adjoint_call(place, mine, came, skew_params)
    parts = exchange(pack)
    next_a, last_b = merge_call(next_a, far_a, last_b, far_b)
    parts, next_a, last_b = lax.optimization_barrier((parts, next_a, last_b))
    slices = sum_call(parts)
    slices, last_a, next_b = lax.optimization_barrier((slices, last_a, next_b))
    next_a = lax.ppermute(next_a, "y", turn(Y, 1))
    last_b = lax.ppermute(last_b, "y", turn(Y, -1))
    others = [lax.ppermute(slices, "y", turn(Y, s)) for s in (1, 2, 3)]
    slices = (slices + others[1]) + (others[0] + others[2])
    routed = route_call(block_owner, place, slices, lax.ppermute(slices, "core", turn(CORES, 1)))
    owned = exchange(routed)
    scale = 1.0 / math.sqrt(cotangent.shape[0] * X * Z * CORES)
    skew_grads = unpack_call(owned, scale)
    input_grad = finish_call(own, next_a, last_a, next_b, last_b)
    return (input_grad, skew_grads)


def solution(mesh):
    grid = Mesh(mesh.devices.reshape(X, Z, CORES, Y), ("x", "z", "core", "y"))
    dp = ("x", "z", "core")
    placed = (P(dp, None), P(dp, "y"), P(None, "y"), P(), P(), P())
    return jax.shard_map(
        local,
        mesh=grid,
        in_specs=placed,
        out_specs=(P(dp, "y"), P(dp, None, None)),
        check_vma=False,
    )
```

```python
import math

import jax
import jax.numpy as jnp
from jax import lax
from jax.experimental import pallas as pl
from jax.experimental.pallas import tpu as pltpu
from jax.sharding import Mesh
from jax.sharding import PartitionSpec as P

SLOTS = 3
FINISH = 10**10
MERGE = 10**10
X, Z, CORES, Y = 4, 8, 2, 4
TILE = 128
BLOCK = 256
f32 = jnp.float32
bf16 = jnp.bfloat16
NN = (((1,), (0,)), ((), ()))
NT = (((1,), (1,)), ((), ()))
TN = (((0,), (0,)), ((), ()))


def dot(a, b, dims=NN):
    return lax.dot_general(a, b, dims, preferred_element_type=f32)


def split(a):
    high = a.astype(bf16)
    return high, (a - high.astype(f32)).astype(bf16)


def stack(a, axis):
    return jnp.concatenate([a[0], a[0], a[1]] if axis else [a[0], a[1], a[0]], axis=axis)


def product(a, b):
    return dot(stack(a, 1), stack(b, 0))


def turned_skew(ref, b):
    plain = ref[b].astype(f32)
    return plain.T - plain


def grad_kernel(
    order, place, weight, cot_t, inputs, skew, turn_high, turn_low, high, low, mine, other,
    skews, tiles, cots, cot, ins, weight_sems, input_sems, sems,
):
    core = place[1]

    def column(t):
        return pl.ds(pl.multiple_of(order[t] * TILE, TILE), TILE)

    def fetch(t):
        return pltpu.make_async_copy(
            weight.at[:, column(t)], tiles.at[t // 2, :, pl.ds(TILE * (t % 2), TILE)], weight_sems.at[t]
        )

    def fetch_inputs(t):
        return pltpu.make_async_copy(
            inputs.at[:, column(t)], ins.at[t // 2, :, pl.ds(TILE * (t % 2), TILE)], input_sems.at[t]
        )

    get_skew = pltpu.make_async_copy(skew, skews, sems.at[0])
    get_cot = pltpu.make_async_copy(cot_t, cots, sems.at[1])
    get_skew.start()
    get_cot.start()
    for t in range(20):
        fetch(t).start()
    for t in range(20):
        fetch_inputs(t).start()
    get_skew.wait()
    rows = lax.broadcasted_iota(jnp.int32, (BLOCK, BLOCK), 0)
    cols = lax.broadcasted_iota(jnp.int32, (BLOCK, BLOCK), 1)
    identity = jnp.where(rows == cols, 1.0, 0.0)
    for b0 in range(0, 10, 5):
        group = range(b0, b0 + 5)
        turned = [turned_skew(skews, b) for b in group]
        pairs = [split(a) for a in turned]
        squares = [product(a, a) for a in pairs]
        cubes = [product(split(a), p) for a, p in zip(squares, pairs)]
        for b, a, square, cube in zip(group, turned, squares, cubes):
            turn_high[b], turn_low[b] = split(identity + 2.0 * a + 2.0 * square + cube)
    get_cot.wait()
    cot[...] = cots[...].T
    for t in range(20):
        fetch(t).wait()
    for b in range(10):
        high[b], low[b] = split(dot(cot[...], tiles[b]))
    for t in range(20):
        fetch_inputs(t).wait()
    for out, first in ((mine, 5 * core), (other, 5 * (1 - core))):
        for j in range(5):
            b = first + j
            tile = ins[b]
            out[j] = dot(tile, high[b], TN) + dot(tile, low[b], TN)


def vmem():
    return pl.BlockSpec(memory_space=pltpu.VMEM)


def smem():
    return pl.BlockSpec(memory_space=pltpu.SMEM)


def anywhere():
    return pl.BlockSpec(memory_space=pltpu.HBM)


def grad_call(tile_order, place, weight_t, cot_t, activations, skew_params):
    wide, tokens = cot_t.shape
    turns = jax.ShapeDtypeStruct((10, BLOCK, BLOCK), bf16)
    part = jax.ShapeDtypeStruct((10, tokens, BLOCK), bf16)
    gram = jax.ShapeDtypeStruct((5, BLOCK, BLOCK), f32)
    return pl.pallas_call(
        grad_kernel,
        out_shape=[turns, turns, part, part, gram, gram],
        in_specs=[smem(), smem()] + [anywhere() for _ in range(4)],
        out_specs=[vmem() for _ in range(6)],
        scratch_shapes=[
            pltpu.VMEM((10, BLOCK, BLOCK), bf16),
            pltpu.VMEM((10, wide, BLOCK), bf16),
            pltpu.VMEM((wide, tokens), bf16),
            pltpu.VMEM((tokens, wide), bf16),
            pltpu.VMEM((10, tokens, BLOCK), bf16),
            pltpu.SemaphoreType.DMA((20,)),
            pltpu.SemaphoreType.DMA((20,)),
            pltpu.SemaphoreType.DMA((2,)),
        ],
        compiler_params=pltpu.CompilerParams(vmem_limit_bytes=40 * 2**20),
        cost_estimate=pl.CostEstimate(flops=8 * 10**9, bytes_accessed=14 * 10**6, transcendentals=0),
        name="grad",
    )(tile_order, place, weight_t, cot_t, activations, skew_params)


def rotate_kernel(order, place, turn_high, turn_low, high, low, far_a, far_b, next_a, next_b, last_a, last_b, own, rotated):
    y = place[0]
    for b in range(10):
        product_b = product((high[b], low[b]), (turn_high[b], turn_low[b]))
        rotated[order[2 * b]] = product_b[:, :TILE]
        rotated[order[2 * b + 1]] = product_b[:, TILE:]
    half = rotated.shape[1] // 2
    for k in range(5):
        own[k] = rotated[5 * y + k]
        for r, (a, b) in enumerate(((next_a, next_b), (far_a, far_b), (last_a, last_b))):
            tile = 5 * lax.rem(y + r + 1, Y) + k
            a[k] = rotated[tile, :half]
            b[k] = rotated[tile, half:]


def rotate_call(tile_order, place, turn_high, turn_low, high, low):
    tokens = high.shape[1]
    half = jax.ShapeDtypeStruct((5, tokens // 2, TILE), f32)
    return pl.pallas_call(
        rotate_kernel,
        out_shape=[half] * 6 + [jax.ShapeDtypeStruct((5, tokens, TILE), f32)],
        in_specs=[smem(), smem()] + [vmem() for _ in range(4)],
        out_specs=[vmem() for _ in range(6)] + [vmem()],
        scratch_shapes=[pltpu.VMEM((20, tokens, TILE), f32)],
        compiler_params=pltpu.CompilerParams(vmem_limit_bytes=24 * 2**20),
        cost_estimate=pl.CostEstimate(flops=2 * 10**9, bytes_accessed=10 * 10**6, transcendentals=0),
        name="rotate",
    )(tile_order, place, turn_high, turn_low, high, low)


def adjoint_kernel(place, mine, came, skew, out):
    core = place[1]
    rows = lax.broadcasted_iota(jnp.int32, (TILE, TILE), 0)
    cols = lax.broadcasted_iota(jnp.int32, (TILE, TILE), 1)
    group = range(5)
    turned = [split(turned_skew(skew, 5 * core + j)) for j in group]
    grams = [mine[j] + came[j] for j in group]
    odd = [a - a.T for a in grams]
    even = [2.0 * (a + a.T) for a in grams]
    first = [product(split(a), t) for a, t in zip(odd, turned)]
    second = [product(split(e + a), t) for e, a, t in zip(even, first, turned)]
    third = [product(t, split(a)) for a, t in zip(first, turned)]
    for j in group:
        total = odd[j] + second[j] + 0.5 * third[j]
        grads = total - total.T
        out[:, j] = jnp.concatenate(
            [jnp.where(rows < cols, grads[:TILE, :TILE], grads[TILE:, TILE:]), grads[:TILE, TILE:]], axis=0
        ).reshape(32, 8, TILE)


def adjoint_call(place, mine, came, skew_params):
    return pl.pallas_call(
        adjoint_kernel,
        out_shape=jax.ShapeDtypeStruct((32, 5, 8, TILE), f32),
        in_specs=[smem()] + [vmem() for _ in range(3)],
        out_specs=vmem(),
        compiler_params=pltpu.CompilerParams(vmem_limit_bytes=20 * 2**20),
        cost_estimate=pl.CostEstimate(flops=2 * 10**9, bytes_accessed=4 * 10**6, transcendentals=0),
        name="adjoint",
    )(place, mine, came, skew_params)


def merge_kernel(next_a, far_a, last_b, far_b, out_a, out_b):
    out_a[...] = next_a[...] + far_a[...]
    out_b[...] = last_b[...] + far_b[...]


def merge_call(*parts):
    return pl.pallas_call(
        merge_kernel,
        out_shape=[jax.ShapeDtypeStruct(parts[0].shape, f32)] * 2,
        in_specs=[vmem() for _ in range(4)],
        out_specs=[vmem() for _ in range(2)],
        compiler_params=pltpu.CompilerParams(vmem_limit_bytes=4 * 2**20),
        cost_estimate=pl.CostEstimate(flops=MERGE, bytes_accessed=4 * 10**6, transcendentals=0),
        name="merge",
    )(*parts)


def sum_kernel(parts, out):
    total = parts[0]
    for i in range(1, 32):
        total = total + parts[i]
    out[...] = total


def sum_call(parts):
    return pl.pallas_call(
        sum_kernel,
        out_shape=jax.ShapeDtypeStruct(parts.shape[1:], f32),
        cost_estimate=pl.CostEstimate(flops=10**6, bytes_accessed=10**6, transcendentals=0),
        name="slice_sum",
    )(parts)


def route_kernel(owner, place, own, other, out):
    core = place[1]
    out[...] = jnp.zeros_like(out)
    for b in range(10):
        target = owner[b]
        rank = jnp.int32(0)
        for e in range(b):
            rank = rank + jnp.where(owner[e] == target, 1, 0)
        side, j = b // 5, b % 5

        @pl.when(lax.rem(target, CORES) == core)
        def _(target=target, rank=rank, side=side, j=j):
            value = jnp.where(core == side, own[j], other[j])
            out[lax.div(target, CORES), rank] = value


def route_call(block_owner, place, own, other):
    return pl.pallas_call(
        route_kernel,
        out_shape=jax.ShapeDtypeStruct((32, SLOTS, 8, TILE), f32),
        in_specs=[smem(), smem(), vmem(), vmem()],
        out_specs=vmem(),
        cost_estimate=pl.CostEstimate(flops=10**5, bytes_accessed=10**6, transcendentals=0),
        name="route",
    )(block_owner, place, own, other)


def unpack_kernel(scale, parts, out):
    rows = lax.broadcasted_iota(jnp.int32, (TILE, TILE), 0)
    cols = lax.broadcasted_iota(jnp.int32, (TILE, TILE), 1)
    for s in range(SLOTS):
        pack = parts[:, s].reshape(2 * TILE, TILE) * scale
        upper = jnp.where(rows < cols, pack[:TILE], 0.0)
        lower = jnp.where(rows > cols, pack[:TILE], 0.0)
        across = pack[TILE:]
        out[s, :TILE, :TILE] = upper - upper.T
        out[s, TILE:, TILE:] = lower - lower.T
        out[s, :TILE, TILE:] = across
        out[s, TILE:, :TILE] = -across.T


def unpack_call(parts, scale):
    return pl.pallas_call(
        lambda parts, out: unpack_kernel(scale, parts, out),
        out_shape=jax.ShapeDtypeStruct((SLOTS, BLOCK, BLOCK), f32),
        in_specs=[vmem()],
        cost_estimate=pl.CostEstimate(flops=10**6, bytes_accessed=10**6, transcendentals=0),
        name="unpack",
    )(parts)


def finish_kernel(own, a1, a2, b1, b2, out):
    half = own.shape[1] // 2
    for k in range(5):
        columns = slice(k * TILE, (k + 1) * TILE)
        out[:half, columns] = (own[k, :half] + a1[k] + a2[k]).astype(bf16)
        out[half:, columns] = (own[k, half:] + b1[k] + b2[k]).astype(bf16)


def finish_call(*parts):
    return pl.pallas_call(
        finish_kernel,
        out_shape=jax.ShapeDtypeStruct((parts[0].shape[1], 5 * TILE), bf16),
        in_specs=[vmem() for _ in range(5)],
        compiler_params=pltpu.CompilerParams(vmem_limit_bytes=16 * 2**20),
        cost_estimate=pl.CostEstimate(flops=FINISH, bytes_accessed=5 * 10**6, transcendentals=0),
        name="finish",
    )(*parts)


def turn(size, by):
    return [(i, (i + by) % size) for i in range(size)]


def exchange(parts):
    rows = parts.reshape(parts.shape[0], -1, parts.shape[-1])
    return lax.all_to_all(rows, ("x", "z"), 0, 0, tiled=True).reshape(parts.shape)


def local(activations, cotangent, frozen_weight, skew_params, tile_order, block_owner):
    place = jnp.stack([lax.axis_index("y"), lax.axis_index("core")]).astype(jnp.int32)
    turn_high, turn_low, high, low, mine, other = grad_call(
        tile_order, place, frozen_weight.T, cotangent.T, activations, skew_params
    )
    came = lax.ppermute(other, "core", turn(CORES, 1))
    far_a, far_b, next_a, next_b, last_a, last_b, own = rotate_call(
        tile_order, place, turn_high, turn_low, high, low
    )
    far_a = lax.ppermute(far_a, "y", turn(Y, 1))
    far_b = lax.ppermute(far_b, "y", turn(Y, -1))
    last_a = lax.ppermute(last_a, "y", turn(Y, -1))
    next_b = lax.ppermute(next_b, "y", turn(Y, 1))
    pack = adjoint_call(place, mine, came, skew_params)
    parts = exchange(pack)
    next_a, last_b = merge_call(next_a, far_a, last_b, far_b)
    parts, next_a, last_b = lax.optimization_barrier((parts, next_a, last_b))
    slices = sum_call(parts)
    others = [lax.ppermute(slices, "y", turn(Y, s)) for s in (1, 2, 3)]
    slices = (slices + others[1]) + (others[0] + others[2])
    slices, next_a, last_b, last_a, next_b = lax.optimization_barrier((slices, next_a, last_b, last_a, next_b))
    next_a = lax.ppermute(next_a, "y", turn(Y, 1))
    last_b = lax.ppermute(last_b, "y", turn(Y, -1))
    routed = route_call(block_owner, place, slices, lax.ppermute(slices, "core", turn(CORES, 1)))
    owned = exchange(routed)
    scale = 1.0 / math.sqrt(cotangent.shape[0] * X * Z * CORES)
    skew_grads = unpack_call(owned, scale)
    input_grad = finish_call(own, next_a, last_a, next_b, last_b)
    return (input_grad, skew_grads)


def solution(mesh):
    grid = Mesh(mesh.devices.reshape(X, Z, CORES, Y), ("x", "z", "core", "y"))
    dp = ("x", "z", "core")
    placed = (P(dp, None), P(dp, "y"), P(None, "y"), P(), P(), P())
    return jax.shard_map(
        local,
        mesh=grid,
        in_specs=placed,
        out_specs=(P(dp, "y"), P(dp, None, None)),
        check_vma=False,
    )
```

```python
import math

import jax
import jax.numpy as jnp
from jax import lax
from jax.experimental import pallas as pl
from jax.experimental.pallas import tpu as pltpu
from jax.sharding import Mesh
from jax.sharding import PartitionSpec as P

SLOTS = 3
FINISH = 10**10
MERGE = 10**10
X, Z, CORES, Y = 4, 8, 2, 4
TILE = 128
BLOCK = 256
f32 = jnp.float32
bf16 = jnp.bfloat16
NN = (((1,), (0,)), ((), ()))
NT = (((1,), (1,)), ((), ()))
TN = (((0,), (0,)), ((), ()))


def dot(a, b, dims=NN):
    return lax.dot_general(a, b, dims, preferred_element_type=f32)


def split(a):
    high = a.astype(bf16)
    return high, (a - high.astype(f32)).astype(bf16)


def stack(a, axis):
    return jnp.concatenate([a[0], a[0], a[1]] if axis else [a[0], a[1], a[0]], axis=axis)


def product(a, b):
    return dot(stack(a, 1), stack(b, 0))


def turned_skew(ref, b):
    plain = ref[b].astype(f32)
    return plain.T - plain


def grad_kernel(
    order, place, weight, cot_t, inputs, skew, turn_high, turn_low, high, low, mine, other,
    skews, tiles, cots, cot, ins, weight_sems, input_sems, sems,
):
    core = place[1]

    def column(t):
        return pl.ds(pl.multiple_of(order[t] * TILE, TILE), TILE)

    def fetch(t):
        return pltpu.make_async_copy(
            weight.at[:, column(t)], tiles.at[t // 2, :, pl.ds(TILE * (t % 2), TILE)], weight_sems.at[t]
        )

    def fetch_inputs(t):
        return pltpu.make_async_copy(
            inputs.at[:, column(t)], ins.at[t // 2, :, pl.ds(TILE * (t % 2), TILE)], input_sems.at[t]
        )

    get_skew = pltpu.make_async_copy(skew, skews, sems.at[0])
    get_cot = pltpu.make_async_copy(cot_t, cots, sems.at[1])
    get_skew.start()
    get_cot.start()
    for t in range(20):
        fetch(t).start()
    for t in range(20):
        fetch_inputs(t).start()
    get_skew.wait()
    rows = lax.broadcasted_iota(jnp.int32, (BLOCK, BLOCK), 0)
    cols = lax.broadcasted_iota(jnp.int32, (BLOCK, BLOCK), 1)
    identity = jnp.where(rows == cols, 1.0, 0.0)
    for b0 in range(0, 10, 5):
        group = range(b0, b0 + 5)
        turned = [turned_skew(skews, b) for b in group]
        pairs = [split(a) for a in turned]
        squares = [product(a, a) for a in pairs]
        cubes = [product(split(a), p) for a, p in zip(squares, pairs)]
        for b, a, square, cube in zip(group, turned, squares, cubes):
            turn_high[b], turn_low[b] = split(identity + 2.0 * a + 2.0 * square + cube)
    get_cot.wait()
    cot[...] = cots[...].T
    for t in range(20):
        fetch(t).wait()
    for b in range(10):
        high[b], low[b] = split(dot(cot[...], tiles[b]))
    for t in range(20):
        fetch_inputs(t).wait()
    for out, first in ((mine, 5 * core), (other, 5 * (1 - core))):
        for j in range(5):
            b = first + j
            tile = ins[b]
            out[j] = dot(tile, high[b], TN) + dot(tile, low[b], TN)


def vmem():
    return pl.BlockSpec(memory_space=pltpu.VMEM)


def smem():
    return pl.BlockSpec(memory_space=pltpu.SMEM)


def anywhere():
    return pl.BlockSpec(memory_space=pltpu.HBM)


def grad_call(tile_order, place, weight_t, cot_t, activations, skew_params):
    wide, tokens = cot_t.shape
    turns = jax.ShapeDtypeStruct((10, BLOCK, BLOCK), bf16)
    part = jax.ShapeDtypeStruct((10, tokens, BLOCK), bf16)
    gram = jax.ShapeDtypeStruct((5, BLOCK, BLOCK), f32)
    return pl.pallas_call(
        grad_kernel,
        out_shape=[turns, turns, part, part, gram, gram],
        in_specs=[smem(), smem()] + [anywhere() for _ in range(4)],
        out_specs=[vmem() for _ in range(6)],
        scratch_shapes=[
            pltpu.VMEM((10, BLOCK, BLOCK), bf16),
            pltpu.VMEM((10, wide, BLOCK), bf16),
            pltpu.VMEM((wide, tokens), bf16),
            pltpu.VMEM((tokens, wide), bf16),
            pltpu.VMEM((10, tokens, BLOCK), bf16),
            pltpu.SemaphoreType.DMA((20,)),
            pltpu.SemaphoreType.DMA((20,)),
            pltpu.SemaphoreType.DMA((2,)),
        ],
        compiler_params=pltpu.CompilerParams(vmem_limit_bytes=40 * 2**20),
        cost_estimate=pl.CostEstimate(flops=8 * 10**9, bytes_accessed=14 * 10**6, transcendentals=0),
        name="grad",
    )(tile_order, place, weight_t, cot_t, activations, skew_params)


def rotate_kernel(order, place, turn_high, turn_low, high, low, far_a, far_b, next_a, next_b, last_a, last_b, own, rotated):
    y = place[0]
    for b in range(10):
        product_b = product((high[b], low[b]), (turn_high[b], turn_low[b]))
        rotated[order[2 * b]] = product_b[:, :TILE]
        rotated[order[2 * b + 1]] = product_b[:, TILE:]
    half = rotated.shape[1] // 2
    for k in range(5):
        own[k] = rotated[5 * y + k]
        for r, (a, b) in enumerate(((next_a, next_b), (far_a, far_b), (last_a, last_b))):
            tile = 5 * lax.rem(y + r + 1, Y) + k
            a[k] = rotated[tile, :half]
            b[k] = rotated[tile, half:]


def rotate_call(tile_order, place, turn_high, turn_low, high, low):
    tokens = high.shape[1]
    half = jax.ShapeDtypeStruct((5, tokens // 2, TILE), f32)
    return pl.pallas_call(
        rotate_kernel,
        out_shape=[half] * 6 + [jax.ShapeDtypeStruct((5, tokens, TILE), f32)],
        in_specs=[smem(), smem()] + [vmem() for _ in range(4)],
        out_specs=[vmem() for _ in range(6)] + [vmem()],
        scratch_shapes=[pltpu.VMEM((20, tokens, TILE), f32)],
        compiler_params=pltpu.CompilerParams(vmem_limit_bytes=24 * 2**20),
        cost_estimate=pl.CostEstimate(flops=2 * 10**9, bytes_accessed=10 * 10**6, transcendentals=0),
        name="rotate",
    )(tile_order, place, turn_high, turn_low, high, low)


def adjoint_kernel(place, mine, came, skew, out):
    core = place[1]
    rows = lax.broadcasted_iota(jnp.int32, (TILE, TILE), 0)
    cols = lax.broadcasted_iota(jnp.int32, (TILE, TILE), 1)
    group = range(5)
    turned = [split(turned_skew(skew, 5 * core + j)) for j in group]
    grams = [mine[j] + came[j] for j in group]
    odd = [a - a.T for a in grams]
    even = [2.0 * (a + a.T) for a in grams]
    first = [product(split(a), t) for a, t in zip(odd, turned)]
    second = [product(split(e + a), t) for e, a, t in zip(even, first, turned)]
    third = [product(t, split(a)) for a, t in zip(first, turned)]
    for j in group:
        total = odd[j] + second[j] + 0.5 * third[j]
        grads = total - total.T
        out[:, j] = jnp.concatenate(
            [jnp.where(rows < cols, grads[:TILE, :TILE], grads[TILE:, TILE:]), grads[:TILE, TILE:]], axis=0
        ).reshape(32, 8, TILE)


def adjoint_call(place, mine, came, skew_params):
    return pl.pallas_call(
        adjoint_kernel,
        out_shape=jax.ShapeDtypeStruct((32, 5, 8, TILE), f32),
        in_specs=[smem()] + [vmem() for _ in range(3)],
        out_specs=vmem(),
        compiler_params=pltpu.CompilerParams(vmem_limit_bytes=20 * 2**20),
        cost_estimate=pl.CostEstimate(flops=2 * 10**9, bytes_accessed=4 * 10**6, transcendentals=0),
        name="adjoint",
    )(place, mine, came, skew_params)


def merge_kernel(next_a, far_a, last_b, far_b, out_a, out_b):
    out_a[...] = next_a[...] + far_a[...]
    out_b[...] = last_b[...] + far_b[...]


def merge_call(*parts):
    return pl.pallas_call(
        merge_kernel,
        out_shape=[jax.ShapeDtypeStruct(parts[0].shape, f32)] * 2,
        in_specs=[vmem() for _ in range(4)],
        out_specs=[vmem() for _ in range(2)],
        compiler_params=pltpu.CompilerParams(vmem_limit_bytes=4 * 2**20),
        cost_estimate=pl.CostEstimate(flops=MERGE, bytes_accessed=4 * 10**6, transcendentals=0),
        name="merge",
    )(*parts)


def sum_kernel(parts, out):
    total = parts[0]
    for i in range(1, 32):
        total = total + parts[i]
    out[...] = total


def sum_call(parts):
    return pl.pallas_call(
        sum_kernel,
        grid=(5,),
        out_shape=jax.ShapeDtypeStruct(parts.shape[1:], f32),
        in_specs=[pl.BlockSpec((32, 1, 8, TILE), lambda j: (0, j, 0, 0))],
        out_specs=pl.BlockSpec((1, 8, TILE), lambda j: (j, 0, 0)),
        compiler_params=pltpu.CompilerParams(vmem_limit_bytes=4 * 2**20),
        cost_estimate=pl.CostEstimate(flops=10**6, bytes_accessed=10**6, transcendentals=0),
        name="slice_sum",
    )(parts)


def route_kernel(owner, place, own, other, out):
    core = place[1]
    out[...] = jnp.zeros_like(out)
    for b in range(10):
        target = owner[b]
        rank = jnp.int32(0)
        for e in range(b):
            rank = rank + jnp.where(owner[e] == target, 1, 0)
        side, j = b // 5, b % 5

        @pl.when(lax.rem(target, CORES) == core)
        def _(target=target, rank=rank, side=side, j=j):
            value = jnp.where(core == side, own[j], other[j])
            out[lax.div(target, CORES), rank] = value


def route_call(block_owner, place, own, other):
    return pl.pallas_call(
        route_kernel,
        out_shape=jax.ShapeDtypeStruct((32, SLOTS, 8, TILE), f32),
        in_specs=[smem(), smem(), vmem(), vmem()],
        out_specs=vmem(),
        compiler_params=pltpu.CompilerParams(vmem_limit_bytes=4 * 2**20),
        cost_estimate=pl.CostEstimate(flops=10**5, bytes_accessed=10**6, transcendentals=0),
        name="route",
    )(block_owner, place, own, other)


def unpack_kernel(scale, parts, out):
    rows = lax.broadcasted_iota(jnp.int32, (TILE, TILE), 0)
    cols = lax.broadcasted_iota(jnp.int32, (TILE, TILE), 1)
    pack = parts[...].reshape(2 * TILE, TILE) * scale
    upper = jnp.where(rows < cols, pack[:TILE], 0.0)
    lower = jnp.where(rows > cols, pack[:TILE], 0.0)
    across = pack[TILE:]
    out[0, :TILE, :TILE] = upper - upper.T
    out[0, TILE:, TILE:] = lower - lower.T
    out[0, :TILE, TILE:] = across
    out[0, TILE:, :TILE] = -across.T


def unpack_call(parts, scale):
    return pl.pallas_call(
        lambda parts, out: unpack_kernel(scale, parts, out),
        grid=(SLOTS,),
        out_shape=jax.ShapeDtypeStruct((SLOTS, BLOCK, BLOCK), f32),
        in_specs=[pl.BlockSpec((32, 1, 8, TILE), lambda s: (0, s, 0, 0))],
        out_specs=pl.BlockSpec((1, BLOCK, BLOCK), lambda s: (s, 0, 0)),
        compiler_params=pltpu.CompilerParams(vmem_limit_bytes=4 * 2**20),
        cost_estimate=pl.CostEstimate(flops=10**6, bytes_accessed=10**6, transcendentals=0),
        name="unpack",
    )(parts)


def finish_kernel(own, a1, a2, b1, b2, out):
    half = own.shape[1] // 2
    for k in range(5):
        columns = slice(k * TILE, (k + 1) * TILE)
        out[:half, columns] = (own[k, :half] + a1[k] + a2[k]).astype(bf16)
        out[half:, columns] = (own[k, half:] + b1[k] + b2[k]).astype(bf16)


def finish_call(*parts):
    return pl.pallas_call(
        finish_kernel,
        out_shape=jax.ShapeDtypeStruct((parts[0].shape[1], 5 * TILE), bf16),
        in_specs=[vmem() for _ in range(5)],
        compiler_params=pltpu.CompilerParams(vmem_limit_bytes=16 * 2**20),
        cost_estimate=pl.CostEstimate(flops=FINISH, bytes_accessed=5 * 10**6, transcendentals=0),
        name="finish",
    )(*parts)


def turn(size, by):
    return [(i, (i + by) % size) for i in range(size)]


def exchange(parts):
    rows = parts.reshape(parts.shape[0], -1, parts.shape[-1])
    return lax.all_to_all(rows, ("x", "z"), 0, 0, tiled=True).reshape(parts.shape)


def local(activations, cotangent, frozen_weight, skew_params, tile_order, block_owner):
    place = jnp.stack([lax.axis_index("y"), lax.axis_index("core")]).astype(jnp.int32)
    turn_high, turn_low, high, low, mine, other = grad_call(
        tile_order, place, frozen_weight.T, cotangent.T, activations, skew_params
    )
    came = lax.ppermute(other, "core", turn(CORES, 1))
    far_a, far_b, next_a, next_b, last_a, last_b, own = rotate_call(
        tile_order, place, turn_high, turn_low, high, low
    )
    far_a = lax.ppermute(far_a, "y", turn(Y, 1))
    far_b = lax.ppermute(far_b, "y", turn(Y, -1))
    last_a = lax.ppermute(last_a, "y", turn(Y, -1))
    next_b = lax.ppermute(next_b, "y", turn(Y, 1))
    pack = adjoint_call(place, mine, came, skew_params)
    parts = exchange(pack)
    next_a, last_b = merge_call(next_a, far_a, last_b, far_b)
    parts, next_a, last_b = lax.optimization_barrier((parts, next_a, last_b))
    slices = sum_call(parts)
    others = [lax.ppermute(slices, "y", turn(Y, s)) for s in (1, 2, 3)]
    slices = (slices + others[1]) + (others[0] + others[2])
    slices, next_a, last_b, last_a, next_b = lax.optimization_barrier((slices, next_a, last_b, last_a, next_b))
    next_a = lax.ppermute(next_a, "y", turn(Y, 1))
    last_b = lax.ppermute(last_b, "y", turn(Y, -1))
    routed = route_call(block_owner, place, slices, lax.ppermute(slices, "core", turn(CORES, 1)))
    owned = exchange(routed)
    scale = 1.0 / math.sqrt(cotangent.shape[0] * X * Z * CORES)
    skew_grads = unpack_call(owned, scale)
    input_grad = finish_call(own, next_a, last_a, next_b, last_b)
    return (input_grad, skew_grads)


def solution(mesh):
    grid = Mesh(mesh.devices.reshape(X, Z, CORES, Y), ("x", "z", "core", "y"))
    dp = ("x", "z", "core")
    placed = (P(dp, None), P(dp, "y"), P(None, "y"), P(), P(), P())
    return jax.shard_map(
        local,
        mesh=grid,
        in_specs=placed,
        out_specs=(P(dp, "y"), P(dp, None, None)),
        check_vma=False,
    )
```

```python
import math

import jax
import jax.numpy as jnp
from jax import lax
from jax.experimental import pallas as pl
from jax.experimental.pallas import tpu as pltpu
from jax.sharding import Mesh
from jax.sharding import PartitionSpec as P

SLOTS = 3
FINISH = 10**10
MERGE = 10**10
X, Z, CORES, Y = 4, 8, 2, 4
TILE = 128
BLOCK = 256
f32 = jnp.float32
bf16 = jnp.bfloat16
NN = (((1,), (0,)), ((), ()))
NT = (((1,), (1,)), ((), ()))
TN = (((0,), (0,)), ((), ()))


def dot(a, b, dims=NN):
    return lax.dot_general(a, b, dims, preferred_element_type=f32)


def split(a):
    high = a.astype(bf16)
    return high, (a - high.astype(f32)).astype(bf16)


def stack(a, axis):
    return jnp.concatenate([a[0], a[0], a[1]] if axis else [a[0], a[1], a[0]], axis=axis)


def product(a, b):
    return dot(stack(a, 1), stack(b, 0))


def square_of(a):
    mixed = dot(a[0], a[1])
    return dot(a[0], a[0]) + (mixed + mixed.T)


def turned_skew(ref, b):
    plain = ref[b].astype(f32)
    return plain.T - plain


def grad_kernel(
    order, place, weight, cot_t, inputs, skew, turn_high, turn_low, high, low, mine, other,
    skews, tiles, cots, cot, ins, weight_sems, input_sems, sems,
):
    core = place[1]

    def column(t):
        return pl.ds(pl.multiple_of(order[t] * TILE, TILE), TILE)

    def fetch(t):
        return pltpu.make_async_copy(
            weight.at[:, column(t)], tiles.at[t // 2, :, pl.ds(TILE * (t % 2), TILE)], weight_sems.at[t]
        )

    def fetch_inputs(t):
        return pltpu.make_async_copy(
            inputs.at[:, column(t)], ins.at[t // 2, :, pl.ds(TILE * (t % 2), TILE)], input_sems.at[t]
        )

    get_skew = pltpu.make_async_copy(skew, skews, sems.at[0])
    get_cot = pltpu.make_async_copy(cot_t, cots, sems.at[1])
    get_skew.start()
    get_cot.start()
    for t in range(20):
        fetch(t).start()
    for t in range(20):
        fetch_inputs(t).start()
    get_skew.wait()
    rows = lax.broadcasted_iota(jnp.int32, (BLOCK, BLOCK), 0)
    cols = lax.broadcasted_iota(jnp.int32, (BLOCK, BLOCK), 1)
    identity = jnp.where(rows == cols, 1.0, 0.0)
    for b0 in range(0, 10, 5):
        group = range(b0, b0 + 5)
        turned = [turned_skew(skews, b) for b in group]
        pairs = [split(a) for a in turned]
        squares = [square_of(a) for a in pairs]
        cubes = [product(split(a), p) for a, p in zip(squares, pairs)]
        for b, a, square, cube in zip(group, turned, squares, cubes):
            turn_high[b], turn_low[b] = split(identity + 2.0 * a + 2.0 * square + cube)
    get_cot.wait()
    cot[...] = cots[...].T
    for b0 in range(0, 10, 5):
        for t in range(2 * b0, 2 * b0 + 10):
            fetch(t).wait()
        for b in range(b0, b0 + 5):
            high[b], low[b] = split(dot(cot[...], tiles[b]))
    for t in range(20):
        fetch_inputs(t).wait()
    for out, first in ((mine, 5 * core), (other, 5 * (1 - core))):
        for j in range(5):
            b = first + j
            tile = ins[b]
            out[j] = dot(tile, high[b], TN) + dot(tile, low[b], TN)


def vmem():
    return pl.BlockSpec(memory_space=pltpu.VMEM)


def smem():
    return pl.BlockSpec(memory_space=pltpu.SMEM)


def anywhere():
    return pl.BlockSpec(memory_space=pltpu.HBM)


def grad_call(tile_order, place, weight_t, cot_t, activations, skew_params):
    wide, tokens = cot_t.shape
    turns = jax.ShapeDtypeStruct((10, BLOCK, BLOCK), bf16)
    part = jax.ShapeDtypeStruct((10, tokens, BLOCK), bf16)
    gram = jax.ShapeDtypeStruct((5, BLOCK, BLOCK), f32)
    return pl.pallas_call(
        grad_kernel,
        out_shape=[turns, turns, part, part, gram, gram],
        in_specs=[smem(), smem()] + [anywhere() for _ in range(4)],
        out_specs=[vmem() for _ in range(6)],
        scratch_shapes=[
            pltpu.VMEM((10, BLOCK, BLOCK), bf16),
            pltpu.VMEM((10, wide, BLOCK), bf16),
            pltpu.VMEM((wide, tokens), bf16),
            pltpu.VMEM((tokens, wide), bf16),
            pltpu.VMEM((10, tokens, BLOCK), bf16),
            pltpu.SemaphoreType.DMA((20,)),
            pltpu.SemaphoreType.DMA((20,)),
            pltpu.SemaphoreType.DMA((2,)),
        ],
        compiler_params=pltpu.CompilerParams(vmem_limit_bytes=40 * 2**20),
        cost_estimate=pl.CostEstimate(flops=8 * 10**9, bytes_accessed=14 * 10**6, transcendentals=0),
        name="grad",
    )(tile_order, place, weight_t, cot_t, activations, skew_params)


def rotate_kernel(order, place, turn_high, turn_low, high, low, far_a, far_b, next_a, next_b, last_a, last_b, own, rotated):
    y = place[0]
    for b in range(10):
        product_b = product((high[b], low[b]), (turn_high[b], turn_low[b]))
        rotated[order[2 * b]] = product_b[:, :TILE]
        rotated[order[2 * b + 1]] = product_b[:, TILE:]
    half = rotated.shape[1] // 2
    for k in range(5):
        own[k] = rotated[5 * y + k]
        for r, (a, b) in enumerate(((next_a, next_b), (far_a, far_b), (last_a, last_b))):
            tile = 5 * lax.rem(y + r + 1, Y) + k
            a[k] = rotated[tile, :half]
            b[k] = rotated[tile, half:]


def rotate_call(tile_order, place, turn_high, turn_low, high, low):
    tokens = high.shape[1]
    half = jax.ShapeDtypeStruct((5, tokens // 2, TILE), f32)
    return pl.pallas_call(
        rotate_kernel,
        out_shape=[half] * 6 + [jax.ShapeDtypeStruct((5, tokens, TILE), f32)],
        in_specs=[smem(), smem()] + [vmem() for _ in range(4)],
        out_specs=[vmem() for _ in range(6)] + [vmem()],
        scratch_shapes=[pltpu.VMEM((20, tokens, TILE), f32)],
        compiler_params=pltpu.CompilerParams(vmem_limit_bytes=24 * 2**20),
        cost_estimate=pl.CostEstimate(flops=2 * 10**9, bytes_accessed=10 * 10**6, transcendentals=0),
        name="rotate",
    )(tile_order, place, turn_high, turn_low, high, low)


def adjoint_kernel(place, mine, came, skew, out):
    core = place[1]
    rows = lax.broadcasted_iota(jnp.int32, (TILE, TILE), 0)
    cols = lax.broadcasted_iota(jnp.int32, (TILE, TILE), 1)
    group = range(5)
    turned = [split(turned_skew(skew, 5 * core + j)) for j in group]
    grams = [mine[j] + came[j] for j in group]
    odd = [a - a.T for a in grams]
    even = [2.0 * (a + a.T) for a in grams]
    first = [product(split(a), t) for a, t in zip(odd, turned)]
    second = [product(split(e + a + 0.5 * a.T), t) for e, a, t in zip(even, first, turned)]
    for j in group:
        total = odd[j] + second[j]
        grads = total - total.T
        out[:, j] = jnp.concatenate(
            [jnp.where(rows < cols, grads[:TILE, :TILE], grads[TILE:, TILE:]), grads[:TILE, TILE:]], axis=0
        ).reshape(32, 8, TILE)


def adjoint_call(place, mine, came, skew_params):
    return pl.pallas_call(
        adjoint_kernel,
        out_shape=jax.ShapeDtypeStruct((32, 5, 8, TILE), f32),
        in_specs=[smem()] + [vmem() for _ in range(3)],
        out_specs=vmem(),
        compiler_params=pltpu.CompilerParams(vmem_limit_bytes=20 * 2**20),
        cost_estimate=pl.CostEstimate(flops=2 * 10**9, bytes_accessed=4 * 10**6, transcendentals=0),
        name="adjoint",
    )(place, mine, came, skew_params)


def merge_kernel(next_a, far_a, last_b, far_b, out_a, out_b):
    out_a[...] = next_a[...] + far_a[...]
    out_b[...] = last_b[...] + far_b[...]


def merge_call(*parts):
    return pl.pallas_call(
        merge_kernel,
        out_shape=[jax.ShapeDtypeStruct(parts[0].shape, f32)] * 2,
        in_specs=[vmem() for _ in range(4)],
        out_specs=[vmem() for _ in range(2)],
        compiler_params=pltpu.CompilerParams(vmem_limit_bytes=4 * 2**20),
        cost_estimate=pl.CostEstimate(flops=MERGE, bytes_accessed=4 * 10**6, transcendentals=0),
        name="merge",
    )(*parts)


def sum_kernel(parts, out):
    total = parts[0]
    for i in range(1, 32):
        total = total + parts[i]
    out[...] = total


def sum_call(parts):
    return pl.pallas_call(
        sum_kernel,
        grid=(5,),
        out_shape=jax.ShapeDtypeStruct(parts.shape[1:], f32),
        in_specs=[pl.BlockSpec((32, 1, 8, TILE), lambda j: (0, j, 0, 0))],
        out_specs=pl.BlockSpec((1, 8, TILE), lambda j: (j, 0, 0)),
        compiler_params=pltpu.CompilerParams(vmem_limit_bytes=4 * 2**20),
        cost_estimate=pl.CostEstimate(flops=10**6, bytes_accessed=10**6, transcendentals=0),
        name="slice_sum",
    )(parts)


def route_kernel(owner, place, own, other, out):
    core = place[1]
    out[...] = jnp.zeros_like(out)
    for b in range(10):
        target = owner[b]
        rank = jnp.int32(0)
        for e in range(b):
            rank = rank + jnp.where(owner[e] == target, 1, 0)
        side, j = b // 5, b % 5

        @pl.when(lax.rem(target, CORES) == core)
        def _(target=target, rank=rank, side=side, j=j):
            value = jnp.where(core == side, own[j], other[j])
            out[lax.div(target, CORES), rank] = value


def route_call(block_owner, place, own, other):
    return pl.pallas_call(
        route_kernel,
        out_shape=jax.ShapeDtypeStruct((32, SLOTS, 8, TILE), f32),
        in_specs=[smem(), smem(), vmem(), vmem()],
        out_specs=vmem(),
        compiler_params=pltpu.CompilerParams(vmem_limit_bytes=4 * 2**20),
        cost_estimate=pl.CostEstimate(flops=10**5, bytes_accessed=10**6, transcendentals=0),
        name="route",
    )(block_owner, place, own, other)


def unpack_kernel(scale, parts, out):
    rows = lax.broadcasted_iota(jnp.int32, (TILE, TILE), 0)
    cols = lax.broadcasted_iota(jnp.int32, (TILE, TILE), 1)
    pack = parts[...].reshape(2 * TILE, TILE) * scale
    upper = jnp.where(rows < cols, pack[:TILE], 0.0)
    lower = jnp.where(rows > cols, pack[:TILE], 0.0)
    across = pack[TILE:]
    out[0, :TILE, :TILE] = upper - upper.T
    out[0, TILE:, TILE:] = lower - lower.T
    out[0, :TILE, TILE:] = across
    out[0, TILE:, :TILE] = -across.T


def unpack_call(parts, scale):
    return pl.pallas_call(
        lambda parts, out: unpack_kernel(scale, parts, out),
        grid=(SLOTS,),
        out_shape=jax.ShapeDtypeStruct((SLOTS, BLOCK, BLOCK), f32),
        in_specs=[pl.BlockSpec((32, 1, 8, TILE), lambda s: (0, s, 0, 0))],
        out_specs=pl.BlockSpec((1, BLOCK, BLOCK), lambda s: (s, 0, 0)),
        compiler_params=pltpu.CompilerParams(vmem_limit_bytes=4 * 2**20),
        cost_estimate=pl.CostEstimate(flops=10**6, bytes_accessed=10**6, transcendentals=0),
        name="unpack",
    )(parts)


def finish_kernel(own, a1, a2, b1, b2, out):
    half = own.shape[1] // 2
    for k in range(5):
        columns = slice(k * TILE, (k + 1) * TILE)
        out[:half, columns] = (own[k, :half] + a1[k] + a2[k]).astype(bf16)
        out[half:, columns] = (own[k, half:] + b1[k] + b2[k]).astype(bf16)


def finish_call(*parts):
    return pl.pallas_call(
        finish_kernel,
        out_shape=jax.ShapeDtypeStruct((parts[0].shape[1], 5 * TILE), bf16),
        in_specs=[vmem() for _ in range(5)],
        compiler_params=pltpu.CompilerParams(vmem_limit_bytes=16 * 2**20),
        cost_estimate=pl.CostEstimate(flops=FINISH, bytes_accessed=5 * 10**6, transcendentals=0),
        name="finish",
    )(*parts)


def turn(size, by):
    return [(i, (i + by) % size) for i in range(size)]


def exchange(parts):
    rows = parts.reshape(parts.shape[0], -1, parts.shape[-1])
    return lax.all_to_all(rows, ("x", "z"), 0, 0, tiled=True).reshape(parts.shape)


def local(activations, cotangent, frozen_weight, skew_params, tile_order, block_owner):
    place = jnp.stack([lax.axis_index("y"), lax.axis_index("core")]).astype(jnp.int32)
    turn_high, turn_low, high, low, mine, other = grad_call(
        tile_order, place, frozen_weight.T, cotangent.T, activations, skew_params
    )
    came = lax.ppermute(other, "core", turn(CORES, 1))
    far_a, far_b, next_a, next_b, last_a, last_b, own = rotate_call(
        tile_order, place, turn_high, turn_low, high, low
    )
    far_a = lax.ppermute(far_a, "y", turn(Y, 1))
    far_b = lax.ppermute(far_b, "y", turn(Y, -1))
    last_a = lax.ppermute(last_a, "y", turn(Y, -1))
    next_b = lax.ppermute(next_b, "y", turn(Y, 1))
    pack = adjoint_call(place, mine, came, skew_params)
    parts = exchange(pack)
    next_a, last_b = merge_call(next_a, far_a, last_b, far_b)
    parts, next_a, last_b = lax.optimization_barrier((parts, next_a, last_b))
    slices = sum_call(parts)
    others = [lax.ppermute(slices, "y", turn(Y, s)) for s in (1, 2, 3)]
    slices = (slices + others[1]) + (others[0] + others[2])
    slices, next_a, last_b, last_a, next_b = lax.optimization_barrier((slices, next_a, last_b, last_a, next_b))
    next_a = lax.ppermute(next_a, "y", turn(Y, 1))
    last_b = lax.ppermute(last_b, "y", turn(Y, -1))
    routed = route_call(block_owner, place, slices, lax.ppermute(slices, "core", turn(CORES, 1)))
    owned = exchange(routed)
    scale = 1.0 / math.sqrt(cotangent.shape[0] * X * Z * CORES)
    skew_grads = unpack_call(owned, scale)
    input_grad = finish_call(own, next_a, last_a, next_b, last_b)
    return (input_grad, skew_grads)


def solution(mesh):
    grid = Mesh(mesh.devices.reshape(X, Z, CORES, Y), ("x", "z", "core", "y"))
    dp = ("x", "z", "core")
    placed = (P(dp, None), P(dp, "y"), P(None, "y"), P(), P(), P())
    return jax.shard_map(
        local,
        mesh=grid,
        in_specs=placed,
        out_specs=(P(dp, "y"), P(dp, None, None)),
        check_vma=False,
    )
```

```python
import math

import jax
import jax.numpy as jnp
from jax import lax
from jax.experimental import pallas as pl
from jax.experimental.pallas import tpu as pltpu
from jax.sharding import Mesh
from jax.sharding import PartitionSpec as P

SLOTS = 3
FINISH = 10**10
MERGE = 10**10
X, Z, CORES, Y = 4, 8, 2, 4
TILE = 128
BLOCK = 256
f32 = jnp.float32
bf16 = jnp.bfloat16
NN = (((1,), (0,)), ((), ()))
NT = (((1,), (1,)), ((), ()))
TN = (((0,), (0,)), ((), ()))


def dot(a, b, dims=NN):
    return lax.dot_general(a, b, dims, preferred_element_type=f32)


def split(a):
    high = a.astype(bf16)
    return high, (a - high.astype(f32)).astype(bf16)


def stack(a, axis):
    return jnp.concatenate([a[0], a[0], a[1]] if axis else [a[0], a[1], a[0]], axis=axis)


def product(a, b):
    return dot(stack(a, 1), stack(b, 0))


def square_of(a):
    mixed = dot(a[0], a[1])
    return dot(a[0], a[0]) + (mixed + mixed.T)


def turned_skew(ref, b):
    plain = ref[b].astype(f32)
    return plain.T - plain


def grad_kernel(
    order, place, weight, cot_t, inputs, skew, turn_high, turn_low, high, low, mine, other,
    skews, tiles, cots, cot, ins, weight_sems, input_sems, sems,
):
    core = place[1]

    def column(t):
        return pl.ds(pl.multiple_of(order[t] * TILE, TILE), TILE)

    def fetch(t):
        return pltpu.make_async_copy(
            weight.at[:, column(t)], tiles.at[t // 2, :, pl.ds(TILE * (t % 2), TILE)], weight_sems.at[t]
        )

    def fetch_inputs(t):
        return pltpu.make_async_copy(
            inputs.at[:, column(t)], ins.at[t // 2, :, pl.ds(TILE * (t % 2), TILE)], input_sems.at[t]
        )

    get_skew = pltpu.make_async_copy(skew, skews, sems.at[0])
    get_cot = pltpu.make_async_copy(cot_t, cots, sems.at[1])
    get_skew.start()
    get_cot.start()
    for t in range(20):
        fetch(t).start()
    for t in range(20):
        fetch_inputs(t).start()
    get_skew.wait()
    rows = lax.broadcasted_iota(jnp.int32, (BLOCK, BLOCK), 0)
    cols = lax.broadcasted_iota(jnp.int32, (BLOCK, BLOCK), 1)
    identity = jnp.where(rows == cols, 1.0, 0.0)
    for b0 in range(0, 10, 5):
        group = range(b0, b0 + 5)
        turned = [turned_skew(skews, b) for b in group]
        pairs = [split(a) for a in turned]
        squares = [square_of(a) for a in pairs]
        cubes = [product(split(a), p) for a, p in zip(squares, pairs)]
        for b, a, square, cube in zip(group, turned, squares, cubes):
            turn_high[b], turn_low[b] = split(identity + 2.0 * a + 2.0 * square + cube)
    get_cot.wait()
    cot[...] = cots[...].T
    for b0 in range(0, 10, 2):
        for t in range(2 * b0, 2 * b0 + 4):
            fetch(t).wait()
        for b in range(b0, b0 + 2):
            high[b], low[b] = split(dot(cot[...], tiles[b]))
    for t in range(20):
        fetch_inputs(t).wait()
    for out, first in ((mine, 5 * core), (other, 5 * (1 - core))):
        for j in range(5):
            b = first + j
            tile = ins[b]
            out[j] = dot(tile, high[b], TN) + dot(tile, low[b], TN)


def vmem():
    return pl.BlockSpec(memory_space=pltpu.VMEM)


def smem():
    return pl.BlockSpec(memory_space=pltpu.SMEM)


def anywhere():
    return pl.BlockSpec(memory_space=pltpu.HBM)


def grad_call(tile_order, place, weight_t, cot_t, activations, skew_params):
    wide, tokens = cot_t.shape
    turns = jax.ShapeDtypeStruct((10, BLOCK, BLOCK), bf16)
    part = jax.ShapeDtypeStruct((10, tokens, BLOCK), bf16)
    gram = jax.ShapeDtypeStruct((5, BLOCK, BLOCK), f32)
    return pl.pallas_call(
        grad_kernel,
        out_shape=[turns, turns, part, part, gram, gram],
        in_specs=[smem(), smem()] + [anywhere() for _ in range(4)],
        out_specs=[vmem() for _ in range(6)],
        scratch_shapes=[
            pltpu.VMEM((10, BLOCK, BLOCK), bf16),
            pltpu.VMEM((10, wide, BLOCK), bf16),
            pltpu.VMEM((wide, tokens), bf16),
            pltpu.VMEM((tokens, wide), bf16),
            pltpu.VMEM((10, tokens, BLOCK), bf16),
            pltpu.SemaphoreType.DMA((20,)),
            pltpu.SemaphoreType.DMA((20,)),
            pltpu.SemaphoreType.DMA((2,)),
        ],
        compiler_params=pltpu.CompilerParams(vmem_limit_bytes=40 * 2**20),
        cost_estimate=pl.CostEstimate(flops=8 * 10**9, bytes_accessed=14 * 10**6, transcendentals=0),
        name="grad",
    )(tile_order, place, weight_t, cot_t, activations, skew_params)


def rotate_kernel(order, place, turn_high, turn_low, high, low, far_a, far_b, next_a, next_b, last_a, last_b, own, rotated):
    y = place[0]
    for b in range(10):
        product_b = product((high[b], low[b]), (turn_high[b], turn_low[b]))
        rotated[order[2 * b]] = product_b[:, :TILE]
        rotated[order[2 * b + 1]] = product_b[:, TILE:]
    half = rotated.shape[1] // 2
    for k in range(5):
        own[k] = rotated[5 * y + k]
        for r, (a, b) in enumerate(((next_a, next_b), (far_a, far_b), (last_a, last_b))):
            tile = 5 * lax.rem(y + r + 1, Y) + k
            a[k] = rotated[tile, :half]
            b[k] = rotated[tile, half:]


def rotate_call(tile_order, place, turn_high, turn_low, high, low):
    tokens = high.shape[1]
    half = jax.ShapeDtypeStruct((5, tokens // 2, TILE), f32)
    return pl.pallas_call(
        rotate_kernel,
        out_shape=[half] * 6 + [jax.ShapeDtypeStruct((5, tokens, TILE), f32)],
        in_specs=[smem(), smem()] + [vmem() for _ in range(4)],
        out_specs=[vmem() for _ in range(6)] + [vmem()],
        scratch_shapes=[pltpu.VMEM((20, tokens, TILE), f32)],
        compiler_params=pltpu.CompilerParams(vmem_limit_bytes=24 * 2**20),
        cost_estimate=pl.CostEstimate(flops=2 * 10**9, bytes_accessed=10 * 10**6, transcendentals=0),
        name="rotate",
    )(tile_order, place, turn_high, turn_low, high, low)


def adjoint_kernel(place, mine, came, skew, out):
    core = place[1]
    rows = lax.broadcasted_iota(jnp.int32, (TILE, TILE), 0)
    cols = lax.broadcasted_iota(jnp.int32, (TILE, TILE), 1)
    group = range(5)
    turned = [split(turned_skew(skew, 5 * core + j)) for j in group]
    grams = [mine[j] + came[j] for j in group]
    odd = [a - a.T for a in grams]
    even = [2.0 * (a + a.T) for a in grams]
    first = [product(split(a), t) for a, t in zip(odd, turned)]
    second = [product(split(e + a + 0.5 * a.T), t) for e, a, t in zip(even, first, turned)]
    for j in group:
        total = odd[j] + second[j]
        grads = total - total.T
        out[:, j] = jnp.concatenate(
            [jnp.where(rows < cols, grads[:TILE, :TILE], grads[TILE:, TILE:]), grads[:TILE, TILE:]], axis=0
        ).reshape(32, 8, TILE)


def adjoint_call(place, mine, came, skew_params):
    return pl.pallas_call(
        adjoint_kernel,
        out_shape=jax.ShapeDtypeStruct((32, 5, 8, TILE), f32),
        in_specs=[smem()] + [vmem() for _ in range(3)],
        out_specs=vmem(),
        compiler_params=pltpu.CompilerParams(vmem_limit_bytes=20 * 2**20),
        cost_estimate=pl.CostEstimate(flops=2 * 10**9, bytes_accessed=4 * 10**6, transcendentals=0),
        name="adjoint",
    )(place, mine, came, skew_params)


def merge_kernel(next_a, far_a, last_b, far_b, out_a, out_b):
    out_a[...] = next_a[...] + far_a[...]
    out_b[...] = last_b[...] + far_b[...]


def merge_call(*parts):
    return pl.pallas_call(
        merge_kernel,
        out_shape=[jax.ShapeDtypeStruct(parts[0].shape, f32)] * 2,
        in_specs=[vmem() for _ in range(4)],
        out_specs=[vmem() for _ in range(2)],
        compiler_params=pltpu.CompilerParams(vmem_limit_bytes=4 * 2**20),
        cost_estimate=pl.CostEstimate(flops=MERGE, bytes_accessed=4 * 10**6, transcendentals=0),
        name="merge",
    )(*parts)


def sum_kernel(parts, out):
    total = parts[0]
    for i in range(1, 32):
        total = total + parts[i]
    out[...] = total


def sum_call(parts):
    return pl.pallas_call(
        sum_kernel,
        grid=(5,),
        out_shape=jax.ShapeDtypeStruct(parts.shape[1:], f32),
        in_specs=[pl.BlockSpec((32, 1, 8, TILE), lambda j: (0, j, 0, 0))],
        out_specs=pl.BlockSpec((1, 8, TILE), lambda j: (j, 0, 0)),
        compiler_params=pltpu.CompilerParams(vmem_limit_bytes=4 * 2**20),
        cost_estimate=pl.CostEstimate(flops=10**6, bytes_accessed=10**6, transcendentals=0),
        name="slice_sum",
    )(parts)


def route_kernel(owner, place, own, other, out):
    core = place[1]
    out[...] = jnp.zeros_like(out)
    for b in range(10):
        target = owner[b]
        rank = jnp.int32(0)
        for e in range(b):
            rank = rank + jnp.where(owner[e] == target, 1, 0)
        side, j = b // 5, b % 5

        @pl.when(lax.rem(target, CORES) == core)
        def _(target=target, rank=rank, side=side, j=j):
            value = jnp.where(core == side, own[j], other[j])
            out[lax.div(target, CORES), rank] = value


def route_call(block_owner, place, own, other):
    return pl.pallas_call(
        route_kernel,
        out_shape=jax.ShapeDtypeStruct((32, SLOTS, 8, TILE), f32),
        in_specs=[smem(), smem(), vmem(), vmem()],
        out_specs=vmem(),
        compiler_params=pltpu.CompilerParams(vmem_limit_bytes=4 * 2**20),
        cost_estimate=pl.CostEstimate(flops=10**5, bytes_accessed=10**6, transcendentals=0),
        name="route",
    )(block_owner, place, own, other)


def unpack_kernel(scale, parts, out):
    rows = lax.broadcasted_iota(jnp.int32, (TILE, TILE), 0)
    cols = lax.broadcasted_iota(jnp.int32, (TILE, TILE), 1)
    pack = parts[...].reshape(2 * TILE, TILE) * scale
    upper = jnp.where(rows < cols, pack[:TILE], 0.0)
    lower = jnp.where(rows > cols, pack[:TILE], 0.0)
    across = pack[TILE:]
    out[0, :TILE, :TILE] = upper - upper.T
    out[0, TILE:, TILE:] = lower - lower.T
    out[0, :TILE, TILE:] = across
    out[0, TILE:, :TILE] = -across.T


def unpack_call(parts, scale):
    return pl.pallas_call(
        lambda parts, out: unpack_kernel(scale, parts, out),
        grid=(SLOTS,),
        out_shape=jax.ShapeDtypeStruct((SLOTS, BLOCK, BLOCK), f32),
        in_specs=[pl.BlockSpec((32, 1, 8, TILE), lambda s: (0, s, 0, 0))],
        out_specs=pl.BlockSpec((1, BLOCK, BLOCK), lambda s: (s, 0, 0)),
        compiler_params=pltpu.CompilerParams(vmem_limit_bytes=4 * 2**20),
        cost_estimate=pl.CostEstimate(flops=10**6, bytes_accessed=10**6, transcendentals=0),
        name="unpack",
    )(parts)


def finish_kernel(own, a1, a2, b1, b2, out):
    half = own.shape[1] // 2
    for k in range(5):
        columns = slice(k * TILE, (k + 1) * TILE)
        out[:half, columns] = (own[k, :half] + a1[k] + a2[k]).astype(bf16)
        out[half:, columns] = (own[k, half:] + b1[k] + b2[k]).astype(bf16)


def finish_call(*parts):
    return pl.pallas_call(
        finish_kernel,
        out_shape=jax.ShapeDtypeStruct((parts[0].shape[1], 5 * TILE), bf16),
        in_specs=[vmem() for _ in range(5)],
        compiler_params=pltpu.CompilerParams(vmem_limit_bytes=16 * 2**20),
        cost_estimate=pl.CostEstimate(flops=FINISH, bytes_accessed=5 * 10**6, transcendentals=0),
        name="finish",
    )(*parts)


def turn(size, by):
    return [(i, (i + by) % size) for i in range(size)]


def exchange(parts):
    rows = parts.reshape(parts.shape[0], -1, parts.shape[-1])
    return lax.all_to_all(rows, ("x", "z"), 0, 0, tiled=True).reshape(parts.shape)


def local(activations, cotangent, frozen_weight, skew_params, tile_order, block_owner):
    place = jnp.stack([lax.axis_index("y"), lax.axis_index("core")]).astype(jnp.int32)
    turn_high, turn_low, high, low, mine, other = grad_call(
        tile_order, place, frozen_weight.T, cotangent.T, activations, skew_params
    )
    came = lax.ppermute(other, "core", turn(CORES, 1))
    far_a, far_b, next_a, next_b, last_a, last_b, own = rotate_call(
        tile_order, place, turn_high, turn_low, high, low
    )
    far_a = lax.ppermute(far_a, "y", turn(Y, 1))
    far_b = lax.ppermute(far_b, "y", turn(Y, -1))
    last_a = lax.ppermute(last_a, "y", turn(Y, -1))
    next_b = lax.ppermute(next_b, "y", turn(Y, 1))
    pack = adjoint_call(place, mine, came, skew_params)
    parts = exchange(pack)
    next_a, last_b = merge_call(next_a, far_a, last_b, far_b)
    parts, next_a, last_b = lax.optimization_barrier((parts, next_a, last_b))
    slices = sum_call(parts)
    others = [lax.ppermute(slices, "y", turn(Y, s)) for s in (1, 2, 3)]
    slices = (slices + others[1]) + (others[0] + others[2])
    slices, next_a, last_b, last_a, next_b = lax.optimization_barrier((slices, next_a, last_b, last_a, next_b))
    next_a = lax.ppermute(next_a, "y", turn(Y, 1))
    last_b = lax.ppermute(last_b, "y", turn(Y, -1))
    routed = route_call(block_owner, place, slices, lax.ppermute(slices, "core", turn(CORES, 1)))
    owned = exchange(routed)
    scale = 1.0 / math.sqrt(cotangent.shape[0] * X * Z * CORES)
    skew_grads = unpack_call(owned, scale)
    input_grad = finish_call(own, next_a, last_a, next_b, last_b)
    return (input_grad, skew_grads)


def solution(mesh):
    grid = Mesh(mesh.devices.reshape(X, Z, CORES, Y), ("x", "z", "core", "y"))
    dp = ("x", "z", "core")
    placed = (P(dp, None), P(dp, "y"), P(None, "y"), P(), P(), P())
    return jax.shard_map(
        local,
        mesh=grid,
        in_specs=placed,
        out_specs=(P(dp, "y"), P(dp, None, None)),
        check_vma=False,
    )
```
